128 devices in a mesh: grp: 4 (over x), dev: 32 (over y, z, core).
Axes of the slice: x: 4, y: 4, z: 4, core: 2. Of those that a mesh axis runs over, the one named last changes fastest.
Arguments:
- pair_owner: int32 [8192, 2], P(('grp', 'dev')), may hold values from 0 to 127, all different within a row; in each aligned block of 64 rows (0 to 63, 64 to 127, ...) at most 2 rows name the same one
- pair_atom: int32 [8192, 2], P(('grp', 'dev')), may hold values from 0 to 95
- integrals: bfloat16 [8192, 128, 1024], P(('grp', 'dev')), may hold values from -1.5 to 1.5
- metric_inverse: bfloat16 [8192, 128, 128], P(('grp', 'dev')), may hold values from -0.3 to 3, as said below
- density: bfloat16 [12288, 1024], P(('grp', 'dev')), may hold values from -0.1796875 to 0.1796875
Outputs:
- exchange_diag: float32 [12288, 1024], P(('grp', 'dev'))
The draws below stay inside these ranges and needn't reach their ends.
Inputs may be any that keep to these rules, and one draw needn't show every extreme that they name: `pair_owner`: the two entries of a row differ. Among the 128 entries of one device's rows, no device is named more than 2 times, and some device is named exactly 2 times in every draw. `metric_inverse`: each pair's matrix is symmetric.
All inputs are finite; a program needn't handle non-finite values.
Results may differ from the reference program's by a relative error of at most 0.0039.
Values may be sent and summed in bfloat16 or wider, within the bound.
A program may use at most 192 MiB of HBM per device.

```python
import math
import jax
import jax.numpy as jnp
import numpy as np
from jax import lax

NB = 32
NFIT = 128
PAIR_DEV = 64
ATOM_DEV = 96
NBB = 1024
CAP = 2
NPAIR = 8192
NATOM = 12288
DEVICES = 128


def draw_metric_inverse(key, part):
    key = jax.random.fold_in(key, 11)
    first_key, second_key = jax.random.split(key)
    raw_values = jnp.clip(jax.random.normal(first_key, (NPAIR, NFIT, NFIT), jnp.float32), -4.0, 4.0)
    symmetric = (raw_values + jnp.swapaxes(raw_values, 1, 2)) * (0.3 / math.sqrt(2.0 * NFIT))
    diagonal = jnp.exp(jax.random.uniform(second_key, (NPAIR, NFIT), jnp.float32, 0.0, math.log(3.0)))
    on_diagonal = jnp.eye(NFIT, dtype=bool)[None, :, :]
    return jnp.where(on_diagonal, diagonal[:, :, None], symmetric).astype(jnp.bfloat16)


def touch_ends(drawn, stream_key, least, largest):
    longest = drawn.shape.index(max(drawn.shape))
    spots = []
    for shift in (0, 1):
        where = [jax.random.randint(jax.random.fold_in(stream_key, axis), (), 0, length) for axis, length in enumerate(drawn.shape)]
        where[longest] = (where[longest] + shift) % drawn.shape[longest]
        spots.append(tuple(where))
    return drawn.at[spots[0]].set(least).at[spots[1]].set(largest)


def block_levels(rng, extent, cuts, smallest, largest):
    level, own = 1.0, jax.random.fold_in(rng, 6)
    for dim, shards_of in cuts:
        heights = jnp.exp(jax.random.uniform(jax.random.fold_in(own, dim), (shards_of,), jnp.float32, smallest / len(cuts), largest / len(cuts)))
        level = level * jnp.repeat(heights, extent[dim] // shards_of).reshape([-1 if axis == dim else 1 for axis in range(len(extent))])
    return level


def routed_block(stream_key, own, number, rows, count, top, bound, slope):
    sequence = jax.random.permutation(stream_key, count)
    packed, common = portions_of(count, rows * top, bound, slope, True), portions_of(count, rows * top, bound, slope, False)
    places = jnp.arange(count)

    def named(lengths, turn):
        used = int((lengths > 0).sum())
        fixed = max(1, used // 4)
        moved = fixed + (places - fixed + turn * (used - fixed)) % max(1, count - fixed)
        return jnp.zeros((count,), jnp.int32).at[sequence[jnp.where(places < fixed, places, moved)]].set(jnp.asarray(lengths, jnp.int32))

    lengths = jnp.where(number % 4 == 0, named(packed, number // 4), named(common, number - number // 4 - 1))
    mixed = jax.random.permutation(jax.random.fold_in(own, 3), count)
    donor, receiver = mixed[0:count // 2 * 2:2], mixed[1:count // 2 * 2:2]
    room = jnp.minimum(lengths[donor] - 1, bound - lengths[receiver]) // 2
    room = jnp.where((donor == sequence[0]) | (receiver == sequence[0]) | (lengths[receiver] == 0), 0, jnp.maximum(room, 0))
    moved = jax.random.randint(jax.random.fold_in(own, 4), (count // 2,), 0, 1 << 20) % (room + 1)
    lengths = lengths.at[donor].add(-moved).at[receiver].add(moved)
    members = jnp.searchsorted(jnp.cumsum(lengths), jnp.arange(rows * top), side="right").astype(jnp.int32)
    grid = members.reshape(top, rows).T
    grid = grid[jax.random.permutation(jax.random.fold_in(own, 1), rows)]
    turn = jax.random.randint(jax.random.fold_in(own, 2), (rows, 1), 0, top)
    return jnp.take_along_axis(grid, (jnp.arange(top)[None, :] + turn) % top, axis=1)


def portions_of(number_of, total, limit, lean, full):
    portions = [(1 << 20) // math.isqrt(rank ** lean) + 1 for rank in range(1, number_of + 1)]
    largest = limit if full else min(limit, max(-(-total // number_of), total * portions[0] // sum(portions)))
    least = 1 if total - largest >= number_of - 1 else 0
    holding, surplus = [largest] + [least] * (number_of - 1), total - largest - least * (number_of - 1)
    while surplus > 0:
        free = [i for i in range(1, number_of) if holding[i] < largest] or [i for i in range(1, number_of) if holding[i] < limit]
        whole, remaining = sum([portions[i] for i in free]), surplus
        for i in free:
            addition = min(limit - holding[i], max(1, remaining * portions[i] // whole), surplus)
            holding[i] = holding[i] + addition
            surplus = surplus - addition
    return np.array(holding)


def gaussian(rng, dims, scale, reach, shards=(), kind=jnp.bfloat16):
    loudness = block_levels(rng, dims, shards, -0.22, 0.18) if shards else 1.0
    drawn = jax.random.normal(rng, dims, jnp.float32) * scale * loudness
    return jnp.minimum(jnp.maximum(drawn, -reach), reach).astype(kind)


def setup_inputs(seed: int = 0) -> dict:
    streams_of = jax.random.split(jax.random.key(seed), 6)
    pair_owner_keys = jax.random.split(jax.random.fold_in(streams_of[0], 1), NPAIR // PAIR_DEV)
    pair_owner_turns = jax.random.permutation(jax.random.fold_in(streams_of[0], 3), NPAIR // PAIR_DEV)
    pair_owner = jax.vmap(lambda own, number: routed_block(jax.random.fold_in(streams_of[0], 2), own, number, PAIR_DEV, DEVICES, 2, CAP, 2))(pair_owner_keys, pair_owner_turns).reshape((NPAIR, 2))
    pair_atom = touch_ends(jax.random.randint(streams_of[1], (NPAIR, 2), 0, ATOM_DEV), jax.random.fold_in(streams_of[1], 1), 0, ATOM_DEV - 1).astype(jnp.int32)
    integrals = gaussian(streams_of[2], (NPAIR, NFIT, NBB), 0.25, 1.5, ((0, 128),))
    metric_inverse = draw_metric_inverse(jax.random.fold_in(streams_of[5], 71), 0)
    density = gaussian(streams_of[4], (NATOM, NBB), 0.03, 0.1796875, ((0, 128),))
    return dict(pair_owner=pair_owner, pair_atom=pair_atom, integrals=integrals, metric_inverse=metric_inverse, density=density)


def rounded(values):
    return lax.optimization_barrier(values.astype(jnp.bfloat16)).astype(jnp.float32)


def reference(pair_owner, pair_atom, integrals, metric_inverse, density):
    atom_ids = (pair_owner * ATOM_DEV + pair_atom).astype(jnp.int32)
    atom_blocks = atom_ids.reshape(DEVICES, PAIR_DEV, 2)
    integral_blocks = integrals.reshape(DEVICES, PAIR_DEV, NFIT, NB * NB)
    metric_blocks = metric_inverse.reshape(DEVICES, PAIR_DEV, NFIT, NFIT)

    def accumulate(totals, inputs):
        block_ids, block_q, block_m = inputs
        q_float = block_q.astype(jnp.float32)
        fitted = rounded(jnp.einsum("pqk,prq->pkr", q_float, block_m.astype(jnp.float32)))
        fitted = fitted.reshape(PAIR_DEV, NB, NB, NFIT)
        first_block = density[block_ids[:, 0]].astype(jnp.float32).reshape(PAIR_DEV, NB, NB)
        second_block = density[block_ids[:, 1]].astype(jnp.float32).reshape(PAIR_DEV, NB, NB)
        q_four = q_float.reshape(PAIR_DEV, NFIT, NB, NB)
        left_part = rounded(jnp.einsum("pmnr,pnk->pmkr", fitted, second_block))
        right_part = rounded(jnp.einsum("pmnr,pml->pnlr", fitted, first_block))
        first_term = jnp.einsum("pmkr,prlk->pml", left_part, q_four).reshape(PAIR_DEV, NB * NB)
        second_term = jnp.einsum("pnlr,prlk->pnk", right_part, q_four).reshape(PAIR_DEV, NB * NB)
        totals = totals.at[block_ids[:, 0]].add(first_term)
        totals = totals.at[block_ids[:, 1]].add(second_term)
        return totals, None

    start = jnp.zeros((NATOM, NB * NB), jnp.float32)
    totals, _ = lax.scan(accumulate, start, (atom_blocks, integral_blocks, metric_blocks))
    return totals
```

```python
import jax
import jax.numpy as jnp
from jax import lax
from jax.experimental import pallas as pl
from jax.experimental.pallas import tpu as pltpu
from jax.sharding import PartitionSpec as P

NB = 32
NFIT = 128
ATOMS = 96
PAIRS = 64
DEVS = 128
GROUP = 4
PITCH = 40
BF16 = jnp.bfloat16
F32 = jnp.float32
MESH = pl.DeviceIdType.MESH
NT = (((1,), (1,)), ((), ()))


def place(t):
    return (t // 32, t % 32)


def my_index():
    return lax.axis_index("grp") * 32 + lax.axis_index("dev")


def greet_all(me):
    barrier = pltpu.get_barrier_semaphore()

    def signal(i, carry):
        pl.semaphore_signal(barrier, inc=1, device_id=place((me + i) % DEVS), device_id_type=MESH)
        return carry

    lax.fori_loop(1, DEVS, signal, 0)
    pl.semaphore_wait(barrier, DEVS - 1)


def swap_blocks(me, send, recv, send_sem, recv_sem):
    own = pltpu.make_async_copy(send.at[me], recv.at[me], recv_sem)
    own.start()

    def start(i, carry):
        t = (me + i) % DEVS
        pltpu.make_async_remote_copy(
            src_ref=send.at[t], dst_ref=recv.at[me], send_sem=send_sem, recv_sem=recv_sem,
            device_id=place(t), device_id_type=MESH,
        ).start()
        return carry

    lax.fori_loop(1, DEVS, start, 0)
    pltpu.make_async_copy(recv, recv, recv_sem).wait()
    others = send.at[pl.ds(0, DEVS - 1)]
    pltpu.make_async_copy(others, others, send_sem).wait()


def fetch_kernel(codes, density, replies, chosen, req, outgoing, landed, rows32, sems):
    me = my_index()
    greet_all(me)
    own = pltpu.make_async_copy(codes, req.at[pl.ds(me, 1)], sems.at[0])
    own.start()

    def start(i, carry):
        t = (me + i) % DEVS
        pltpu.make_async_remote_copy(
            src_ref=codes, dst_ref=req.at[pl.ds(me, 1)], send_sem=sems.at[1], recv_sem=sems.at[0],
            device_id=place(t), device_id_type=MESH,
        ).start()
        return carry

    lax.fori_loop(1, DEVS, start, 0)
    pltpu.make_async_copy(req, req, sems.at[0]).wait()
    others = req.at[pl.ds(0, DEVS - 1)]
    pltpu.make_async_copy(others, others, sems.at[1]).wait()

    local = req[...] - ATOMS * me
    mine = (local >= 0) & (local < ATOMS)
    coded = lax.broadcasted_iota(jnp.int32, (DEVS, 128), 1) * 128 + local
    first = jnp.min(jnp.where(mine, coded, 128 * 128 - 1), axis=1, keepdims=True) % 128
    last = jnp.max(jnp.where(mine, coded, 127), axis=1, keepdims=True) % 128
    atoms = lax.broadcasted_iota(jnp.int32, (DEVS, 128), 1)
    for c, atom in enumerate((first, last)):
        onehot = jnp.where(atoms == atom, 1.0, 0.0)
        chosen[c] = onehot.T.astype(BF16)
        picks = onehot[:, :ATOMS].astype(BF16)
        for part in range(8):
            rows32[pl.ds(8 * c + part, DEVS, stride=16), :] = jnp.dot(
                picks, density[:, part * 128 : (part + 1) * 128], preferred_element_type=F32
            )
    outgoing[...] = rows32[...].reshape(DEVS, 16, 128).astype(BF16)
    swap_blocks(me, outgoing, landed, sems.at[2], sems.at[3])
    replies[...] = landed[...]


def return_kernel(outbox, chosen, total, landed, rows32, sems):
    me = my_index()
    greet_all(me)
    swap_blocks(me, outbox, landed, sems.at[0], sems.at[1])
    rows32[...] = landed[...].astype(F32).reshape(DEVS * 16, 128)
    for part in range(8):
        acc = None
        for c in range(2):
            tile = rows32[pl.ds(8 * c + part, DEVS, stride=16), :].astype(BF16)
            term = jnp.dot(chosen[c, :ATOMS, :], tile, preferred_element_type=F32)
            acc = term if acc is None else acc + term
        total[:, part * 128 : (part + 1) * 128] = acc


def spread(block, lane_group):
    return jnp.concatenate([jnp.where(lane_group == g, block, 0.0) for g in range(4)], axis=0).astype(BF16)


def eightfold(e_ref, keep):
    rows = [jnp.where(keep, jnp.broadcast_to(e_ref[c : c + 1, :], (8, 256)), 0.0) for c in range(NB)]
    return jnp.concatenate(rows, axis=0).astype(BF16)


def apply_block(k, w_ref, rows, y_ref, where_a, where_c):
    w = jnp.concatenate(
        [
            jnp.concatenate(
                [w_ref[rows, where_a(ac, a) * 128 : (where_a(ac, a) + 1) * 128] for a in range(8)], axis=0
            )
            for ac in range(4)
        ],
        axis=1,
    )
    y = jnp.dot(k, w, preferred_element_type=F32)
    for c in range(NB):
        at = where_c(c)
        y_ref[rows, at * 128 : (at + 1) * 128] = jnp.concatenate(
            [y[c * 8 : (c + 1) * 8, ac * 128 : (ac + 1) * 128] for ac in range(4)], axis=0
        ).astype(BF16)


def pair_kernel(owner, slot, q_ref, m_ref, replies, outbox, z_ref, fw, qw, x_ref, r_ref, e1_ref, e2_ref, boxes):
    step = pl.program_id(0)

    @pl.when(step == 0)
    def _():
        boxes[...] = jnp.zeros_like(boxes)

    lane256 = lax.broadcasted_iota(jnp.int32, (8, 256), 1)
    keep = lax.broadcasted_iota(jnp.int32, (8, 256), 0) == lane256 // NB
    lane_group = lax.broadcasted_iota(jnp.int32, (8, 128), 1) // NB
    tile8 = jnp.where(
        lax.broadcasted_iota(jnp.int32, (128, 256), 0) % NB == lax.broadcasted_iota(jnp.int32, (128, 256), 1) % NB,
        1.0, 0.0,
    ).astype(BF16)
    pick = jnp.where(
        lax.broadcasted_iota(jnp.int32, (NB, 128), 0) == lax.broadcasted_iota(jnp.int32, (NB, 128), 1) % NB, 1.0, 0.0
    ).astype(BF16)

    def fetched(item):
        both = replies[owner[item]].astype(F32)
        return jnp.where(slot[item] == 0, both[:8], both[8:])

    for p in range(GROUP):
        rows = slice(p * NB, (p + 1) * NB)
        for c in range(8):
            t = q_ref[p, :, c * 128 : (c + 1) * 128].T
            y = jnp.dot(t, m_ref[p], preferred_element_type=F32)
            for j in range(4):
                m = 4 * c + j
                qw[rows, m * 128 : (m + 1) * 128] = t[j * NB : (j + 1) * NB]
                z_ref[p, m * PITCH : m * PITCH + NB, :] = y[j * NB : (j + 1) * NB]
        for n in range(NB):
            fw[rows, n * 128 : (n + 1) * 128] = jnp.concatenate(
                [z_ref[p, pl.ds(g * PITCH + n, 8, stride=4 * PITCH), :] for g in range(4)], axis=0
            ).astype(BF16)
        first_density = spread(fetched(step * GROUP + p), lane_group)
        second_density = spread(fetched(PAIRS + step * GROUP + p), lane_group)
        e2_ref[p] = jnp.dot(second_density, tile8, preferred_element_type=F32)
        e1_ref[p] = lax.dot_general(
            pick, jnp.concatenate([first_density] * 8, axis=0), NT, preferred_element_type=F32
        )
        apply_block(
            eightfold(e2_ref.at[p], keep), qw, rows, x_ref, lambda ac, a: ac * 8 + a, lambda c: (c % 8) * 4 + c // 8
        )
        apply_block(eightfold(e1_ref.at[p], keep), fw, rows, r_ref, lambda ac, a: a * 4 + ac, lambda c: c)
    first = lax.dot_general(fw[...], x_ref[...], NT, preferred_element_type=F32)
    second = lax.dot_general(r_ref[...], qw[...], NT, preferred_element_type=F32)
    for side, gram in ((0, first), (1, second)):
        for p in range(GROUP):
            block = jnp.zeros((8, 128), F32)
            for g in range(4):
                part = gram[p * NB + g * 8 : p * NB + (g + 1) * 8, :]
                turn = ((g - p) % 4) * NB
                block = jnp.where(lane_group == g, part if turn == 0 else pltpu.roll(part, turn, 1), block)
            item = side * PAIRS + step * GROUP + p
            boxes[owner[item], slot[item]] = block

    @pl.when(step == PAIRS // GROUP - 1)
    def _():
        outbox[...] = boxes[...].reshape(DEVS, 16, 128).astype(BF16)


def local(pair_owner, pair_atom, integrals, metric_inverse, density):
    vmem = pl.BlockSpec(memory_space=pltpu.VMEM)
    smem = pl.BlockSpec(memory_space=pltpu.SMEM)
    owner = pair_owner.T.reshape(2 * PAIRS)
    codes = owner * ATOMS + pair_atom.T.reshape(2 * PAIRS)
    earlier = jnp.tril(jnp.ones((2 * PAIRS, 2 * PAIRS), jnp.int32), -1)
    slot = jnp.sum(jnp.where(owner[:, None] == owner[None, :], earlier, 0), axis=1)
    replies, chosen = pl.pallas_call(
        fetch_kernel,
        out_shape=[jax.ShapeDtypeStruct((DEVS, 16, 128), BF16), jax.ShapeDtypeStruct((2, 128, DEVS), BF16)],
        in_specs=[vmem] * 2,
        out_specs=[vmem] * 2,
        scratch_shapes=[
            pltpu.VMEM((DEVS, 128), jnp.int32),
            pltpu.VMEM((DEVS, 16, 128), BF16),
            pltpu.VMEM((DEVS, 16, 128), BF16),
            pltpu.VMEM((DEVS * 16, 128), F32),
            pltpu.SemaphoreType.DMA((4,)),
        ],
        compiler_params=pltpu.CompilerParams(
            collective_id=0, has_side_effects=True, vmem_limit_bytes=32 * 2**20
        ),
        name="fetch",
    )(codes.reshape(1, 2 * PAIRS), density)
    outbox = pl.pallas_call(
        pair_kernel,
        grid=(PAIRS // GROUP,),
        out_shape=jax.ShapeDtypeStruct((DEVS, 16, 128), BF16),
        in_specs=[
            smem,
            smem,
            pl.BlockSpec((GROUP, NFIT, NB * NB), lambda i: (i, 0, 0)),
            pl.BlockSpec((GROUP, NFIT, NFIT), lambda i: (i, 0, 0)),
            pl.BlockSpec((DEVS, 16, 128), lambda i: (0, 0, 0)),
        ],
        out_specs=pl.BlockSpec((DEVS, 16, 128), lambda i: (0, 0, 0)),
        scratch_shapes=[
            pltpu.VMEM((GROUP, NB * PITCH, 128), F32),
            pltpu.VMEM((GROUP * NB, NB * NFIT), BF16),
            pltpu.VMEM((GROUP * NB, NB * NFIT), BF16),
            pltpu.VMEM((GROUP * NB, NB * NFIT), BF16),
            pltpu.VMEM((GROUP * NB, NB * NFIT), BF16),
            pltpu.VMEM((GROUP, NB, 256), F32),
            pltpu.VMEM((GROUP, NB, 256), F32),
            pltpu.VMEM((DEVS, 2, 8, 128), F32),
        ],
        compiler_params=pltpu.CompilerParams(vmem_limit_bytes=48 * 2**20),
        name="pairs",
    )(owner, slot, integrals, metric_inverse, replies)
    return pl.pallas_call(
        return_kernel,
        out_shape=jax.ShapeDtypeStruct((ATOMS, NB * NB), F32),
        in_specs=[vmem] * 2,
        out_specs=vmem,
        scratch_shapes=[
            pltpu.VMEM((DEVS, 16, 128), BF16),
            pltpu.VMEM((DEVS * 16, 128), F32),
            pltpu.SemaphoreType.DMA((2,)),
        ],
        compiler_params=pltpu.CompilerParams(
            collective_id=1, has_side_effects=True, vmem_limit_bytes=32 * 2**20
        ),
        name="give_back",
    )(outbox, chosen)


def solution(mesh):
    placed = (
        P(("grp", "dev"), None),
        P(("grp", "dev"), None),
        P(("grp", "dev"), None, None),
        P(("grp", "dev"), None, None),
        P(("grp", "dev"), None),
    )
    return jax.shard_map(
        local, mesh=mesh, in_specs=placed, out_specs=P(("grp", "dev"), None), check_vma=False
    )
```

```python
import itertools

import jax
import jax.numpy as jnp
from jax import lax
from jax.experimental import pallas as pl
from jax.experimental.pallas import tpu as pltpu
from jax.sharding import PartitionSpec as P

NB = 32
NFIT = 128
ATOMS = 96
PAIRS = 64
DEVS = 128
GROUP = 4
GROUPS = PAIRS // GROUP
BUFFERS = 4
EARLY = 9
EXPAND = 16
PITCH = 33
BF16 = jnp.bfloat16
F32 = jnp.float32
MESH = pl.DeviceIdType.MESH
NT = (((1,), (1,)), ((), ()))


OFFSETS = sorted(
    (o for o in itertools.product(range(4), range(4), range(4), range(2)) if any(o)),
    key=lambda o: (-sum(min(v, 4 - v) for v in o[:3]), -o[3]),
)


def place(t):
    return (t // 32, t % 32)


def my_index():
    return lax.axis_index("grp") * 32 + lax.axis_index("dev")


def farthest_first(me):
    x, y, z, core = me // 32, (me // 8) % 4, (me // 2) % 4, me % 2
    for dx, dy, dz, dc in OFFSETS:
        yield ((x + dx) % 4) * 32 + ((y + dy) % 4) * 8 + ((z + dz) % 4) * 2 + (core + dc) % 2


def start_swap(me, send, recv, send_sem, recv_sem):
    pltpu.make_async_copy(send.at[me], recv.at[me], recv_sem).start()
    for t in farthest_first(me):
        pltpu.make_async_remote_copy(
            src_ref=send.at[t], dst_ref=recv.at[me], send_sem=send_sem, recv_sem=recv_sem,
            device_id=place(t), device_id_type=MESH,
        ).start()


def wait_swap(send, recv, send_sem, recv_sem):
    pltpu.make_async_copy(recv, recv, recv_sem).wait()
    others = send.at[pl.ds(0, DEVS - 1)]
    pltpu.make_async_copy(others, others, send_sem).wait()


def spread(block, lane_group):
    return jnp.concatenate([jnp.where(lane_group == g, block, 0.0) for g in range(4)], axis=0).astype(BF16)


def eightfold(e_ref, keep):
    rows = [jnp.where(keep, jnp.broadcast_to(e_ref[c : c + 1, :], (8, 256)), 0.0) for c in range(NB)]
    return jnp.concatenate(rows, axis=0).astype(BF16)


def apply_block(k, w_ref, g, rows, y_ref, where_a, where_c):
    w = jnp.concatenate(
        [
            jnp.concatenate(
                [w_ref[g, rows, where_a(ac, a) * 128 : (where_a(ac, a) + 1) * 128] for a in range(8)], axis=0
            )
            for ac in range(4)
        ],
        axis=1,
    )
    y = jnp.dot(k, w, preferred_element_type=F32)
    for c in range(NB):
        at = where_c(c)
        y_ref[rows, at * 128 : (at + 1) * 128] = jnp.concatenate(
            [y[c * 8 : (c + 1) * 8, ac * 128 : (ac + 1) * 128] for ac in range(4)], axis=0
        ).astype(BF16)


def item_tables(owner_ref, atom_ref, tables):
    items = 2 * PAIRS
    lane = lax.broadcasted_iota(jnp.int32, (PAIRS, items), 1)
    here = lane % PAIRS == lax.broadcasted_iota(jnp.int32, (PAIRS, items), 0)

    def as_row(ref):
        both = jnp.where(lane < PAIRS, ref[:, 0:1], ref[:, 1:2])
        return jnp.sum(jnp.where(here, both, 0), axis=0, keepdims=True)

    owner = as_row(owner_ref)
    column = jnp.concatenate([owner_ref[:, 0:1], owner_ref[:, 1:2]], axis=0)
    item = lax.broadcasted_iota(jnp.int32, (items, items), 0)
    across = lax.broadcasted_iota(jnp.int32, (items, items), 1)
    slot = jnp.sum(jnp.where((column == owner) & (item < across), 1, 0), axis=0, keepdims=True)
    named = column == across
    first = jnp.min(jnp.where(named, item, items), axis=0, keepdims=True)
    last = jnp.max(jnp.where(named, item, -1), axis=0, keepdims=True)
    tables[0:1, :] = owner * ATOMS + as_row(atom_ref)
    tables[1:2, :] = owner
    tables[2:3, :] = slot
    tables[3:4, :] = first
    tables[4:5, :] = jnp.where(last > first, last, items)
    tables[5:8, :] = jnp.zeros((3, items), jnp.int32)


def exchange_kernel(
    owner_ref, atom_ref, integrals, metric, density, total,
    tables, scalars, req, dens, outgoing, landed, outbox, returned, rows32, chosen,
    q_buf, m_buf, z_ref, fw, qw, x_ref, r_ref, e1_ref, e2_ref, terms,
    sems, q_sems, m_sems,
):
    me = my_index()

    def load(g, buffer):
        return (
            pltpu.make_async_copy(integrals.at[pl.ds(g * GROUP, GROUP)], q_buf.at[buffer], q_sems.at[buffer]),
            pltpu.make_async_copy(metric.at[pl.ds(g * GROUP, GROUP)], m_buf.at[buffer], m_sems.at[buffer]),
        )

    barrier = pltpu.get_barrier_semaphore()

    def signal(i, carry):
        pl.semaphore_signal(barrier, inc=1, device_id=place((me + i) % DEVS), device_id_type=MESH)
        return carry

    lax.fori_loop(1, DEVS, signal, 0)
    for g in range(BUFFERS):
        for copy in load(g, g):
            copy.start()
    density_copy = pltpu.make_async_copy(density, dens, sems.at[4])
    density_copy.start()
    item_tables(owner_ref, atom_ref, tables)
    table_copy = pltpu.make_async_copy(tables, scalars, sems.at[5])
    table_copy.start()
    pl.semaphore_wait(barrier, DEVS - 1)

    codes = tables.at[pl.ds(0, 1)]
    pltpu.make_async_copy(codes, req.at[pl.ds(me, 1)], sems.at[0]).start()
    for t in farthest_first(me):
        pltpu.make_async_remote_copy(
            src_ref=codes, dst_ref=req.at[pl.ds(me, 1)], send_sem=sems.at[1], recv_sem=sems.at[0],
            device_id=place(t), device_id_type=MESH,
        ).start()
    terms[2 * PAIRS] = jnp.zeros((8, 128), F32)

    def fit(g, carry):
        buffer = g % BUFFERS
        for copy in load(g, buffer):
            copy.wait()
        for p in range(GROUP):
            rows = slice(p * NB, (p + 1) * NB)
            for c in range(8):
                t = q_buf[buffer, p, :, c * 128 : (c + 1) * 128].T
                y = jnp.dot(t, m_buf[buffer, p], preferred_element_type=F32)
                for j in range(4):
                    m = 4 * c + j
                    at = (j * 8 + c) * PITCH
                    qw[g, rows, m * 128 : (m + 1) * 128] = t[j * NB : (j + 1) * NB]
                    z_ref[p, at : at + NB, :] = y[j * NB : (j + 1) * NB]
            for n in range(NB):
                fw[g, rows, n * 128 : (n + 1) * 128] = z_ref[p, pl.ds(n, NB, stride=PITCH), :].astype(BF16)

        @pl.when(g + BUFFERS < GROUPS)
        def _():
            for copy in load(g + BUFFERS, buffer):
                copy.start()

        return carry

    lax.fori_loop(0, EARLY, fit, 0)

    pltpu.make_async_copy(req, req, sems.at[0]).wait()
    density_copy.wait()
    local = req[...] - ATOMS * me
    mine = (local >= 0) & (local < ATOMS)
    coded = lax.broadcasted_iota(jnp.int32, (DEVS, 128), 1) * 128 + local
    first = jnp.min(jnp.where(mine, coded, 128 * 128 - 1), axis=1, keepdims=True) % 128
    last = jnp.max(jnp.where(mine, coded, 127), axis=1, keepdims=True) % 128
    atoms = lax.broadcasted_iota(jnp.int32, (DEVS, 128), 1)
    onehots = [jnp.where(atoms == atom, 1.0, 0.0) for atom in (first, last)]
    for c in range(2):
        picks = onehots[c][:, :ATOMS].astype(BF16)
        for part in range(8):
            rows32[pl.ds(8 * c + part, DEVS, stride=16), :] = jnp.dot(
                picks, dens[:, part * 128 : (part + 1) * 128], preferred_element_type=F32
            )
    outgoing[...] = rows32[...].reshape(DEVS, 16, 128).astype(BF16)
    start_swap(me, outgoing, landed, sems.at[2], sems.at[3])
    for c in range(2):
        chosen[c] = onehots[c].T.astype(BF16)
    others = req.at[pl.ds(0, DEVS - 1)]
    pltpu.make_async_copy(others, others, sems.at[1]).wait()
    table_copy.wait()
    lax.fori_loop(EARLY, GROUPS, fit, 0)
    wait_swap(outgoing, landed, sems.at[2], sems.at[3])

    lane256 = lax.broadcasted_iota(jnp.int32, (8, 256), 1)
    keep = lax.broadcasted_iota(jnp.int32, (8, 256), 0) == lane256 // NB
    lane_group = lax.broadcasted_iota(jnp.int32, (8, 128), 1) // NB
    tile8 = jnp.where(
        lax.broadcasted_iota(jnp.int32, (128, 256), 0) % NB == lax.broadcasted_iota(jnp.int32, (128, 256), 1) % NB,
        1.0, 0.0,
    ).astype(BF16)
    pick = jnp.where(
        lax.broadcasted_iota(jnp.int32, (NB, 128), 0) == lax.broadcasted_iota(jnp.int32, (NB, 128), 1) % NB, 1.0, 0.0
    ).astype(BF16)

    def fetched(item):
        both = landed[scalars[1, item]].astype(F32)
        return jnp.where(scalars[2, item] == 0, both[:8], both[8:])

    def expand(h, carry):
        firsts = [spread(fetched(h * EXPAND + p), lane_group) for p in range(EXPAND)]
        seconds = [spread(fetched(PAIRS + h * EXPAND + p), lane_group) for p in range(EXPAND)]
        e2 = jnp.dot(jnp.concatenate(seconds, axis=0), tile8, preferred_element_type=F32)
        e2_ref[pl.ds(h * EXPAND, EXPAND)] = e2.reshape(EXPAND, NB, 256)
        e1 = lax.dot_general(
            pick, jnp.concatenate([f for f in firsts for _ in range(8)], axis=0), NT, preferred_element_type=F32
        )
        for p in range(EXPAND):
            e1_ref[h * EXPAND + p] = e1[:, p * 256 : (p + 1) * 256]
        return carry

    lax.fori_loop(0, PAIRS // EXPAND, expand, 0)

    def contract(g, carry):
        for p in range(GROUP):
            rows = slice(p * NB, (p + 1) * NB)
            pair = g * GROUP + p
            apply_block(
                eightfold(e2_ref.at[pair], keep), qw, g, rows, x_ref,
                lambda ac, a: ac * 8 + a, lambda c: (c % 8) * 4 + c // 8,
            )
            apply_block(
                eightfold(e1_ref.at[pair], keep), fw, g, rows, r_ref, lambda ac, a: a * 4 + ac, lambda c: c
            )
        first_gram = lax.dot_general(fw[g], x_ref[...], NT, preferred_element_type=F32)
        second_gram = lax.dot_general(r_ref[...], qw[g], NT, preferred_element_type=F32)
        for side, gram in ((0, first_gram), (1, second_gram)):
            for p in range(GROUP):
                block = jnp.zeros((8, 128), F32)
                for k in range(4):
                    part = gram[p * NB + k * 8 : p * NB + (k + 1) * 8, :]
                    turn = ((k - p) % 4) * NB
                    block = jnp.where(lane_group == k, part if turn == 0 else pltpu.roll(part, turn, 1), block)
                terms[side * PAIRS + g * GROUP + p] = block
        return carry

    lax.fori_loop(0, GROUPS, contract, 0)

    def box(t, carry):
        both = jnp.concatenate([terms[scalars[3, t]], terms[scalars[4, t]]], axis=0)
        outbox[t] = both.astype(BF16)
        return carry

    lax.fori_loop(0, DEVS, box, 0, unroll=8)
    start_swap(me, outbox, returned, sems.at[6], sems.at[7])
    wait_swap(outbox, returned, sems.at[6], sems.at[7])
    rows32[...] = returned[...].astype(F32).reshape(DEVS * 16, 128)
    for part in range(8):
        acc = None
        for c in range(2):
            tile = rows32[pl.ds(8 * c + part, DEVS, stride=16), :].astype(BF16)
            term = jnp.dot(chosen[c, :ATOMS, :], tile, preferred_element_type=F32)
            acc = term if acc is None else acc + term
        total[:, part * 128 : (part + 1) * 128] = acc


def local(pair_owner, pair_atom, integrals, metric_inverse, density):
    vmem = pl.BlockSpec(memory_space=pltpu.VMEM)
    hbm = pl.BlockSpec(memory_space=pl.ANY)
    boxes = pltpu.VMEM((DEVS, 16, 128), BF16)
    wide = (GROUP * NB, NB * NFIT)
    return pl.pallas_call(
        exchange_kernel,
        out_shape=jax.ShapeDtypeStruct((ATOMS, NB * NB), F32),
        in_specs=[vmem, vmem, hbm, hbm, hbm],
        out_specs=vmem,
        scratch_shapes=[
            pltpu.VMEM((8, 2 * PAIRS), jnp.int32),
            pltpu.SMEM((8, 2 * PAIRS), jnp.int32),
            pltpu.VMEM((DEVS, 2 * PAIRS), jnp.int32),
            pltpu.VMEM((ATOMS, NB * NB), BF16),
            boxes, boxes, boxes, boxes,
            pltpu.VMEM((DEVS * 16, 128), F32),
            pltpu.VMEM((2, 128, DEVS), BF16),
            pltpu.VMEM((BUFFERS, GROUP, NFIT, NB * NB), BF16),
            pltpu.VMEM((BUFFERS, GROUP, NFIT, NFIT), BF16),
            pltpu.VMEM((GROUP, NB * PITCH, 128), F32),
            pltpu.VMEM((GROUPS, *wide), BF16),
            pltpu.VMEM((GROUPS, *wide), BF16),
            pltpu.VMEM(wide, BF16),
            pltpu.VMEM(wide, BF16),
            pltpu.VMEM((PAIRS, NB, 256), F32),
            pltpu.VMEM((PAIRS, NB, 256), F32),
            pltpu.VMEM((2 * PAIRS + 1, 8, 128), F32),
            pltpu.SemaphoreType.DMA((8,)),
            pltpu.SemaphoreType.DMA((BUFFERS,)),
            pltpu.SemaphoreType.DMA((BUFFERS,)),
        ],
        compiler_params=pltpu.CompilerParams(
            collective_id=0, has_side_effects=True, vmem_limit_bytes=58 * 2**20
        ),
        name="exchange",
    )(pair_owner, pair_atom, integrals, metric_inverse, density)


def solution(mesh):
    placed = (
        P(("grp", "dev"), None),
        P(("grp", "dev"), None),
        P(("grp", "dev"), None, None),
        P(("grp", "dev"), None, None),
        P(("grp", "dev"), None),
    )
    return jax.shard_map(
        local, mesh=mesh, in_specs=placed, out_specs=P(("grp", "dev"), None), check_vma=False
    )
```

```python
import itertools

import jax
import jax.numpy as jnp
from jax import lax
from jax.experimental import pallas as pl
from jax.experimental.pallas import tpu as pltpu
from jax.sharding import PartitionSpec as P

NB = 32
NFIT = 128
ATOMS = 96
PAIRS = 64
DEVS = 128
GROUP = 4
GROUPS = PAIRS // GROUP
BUFFERS = 4
EARLY = 9
PITCH = 33
BF16 = jnp.bfloat16
F32 = jnp.float32
MESH = pl.DeviceIdType.MESH
NT = (((1,), (1,)), ((), ()))


OFFSETS = sorted(
    (o for o in itertools.product(range(4), range(4), range(4), range(2)) if any(o)),
    key=lambda o: (-sum(min(v, 4 - v) for v in o[:3]), -o[3]),
)


def place(t):
    return (t // 32, t % 32)


def my_index():
    return lax.axis_index("grp") * 32 + lax.axis_index("dev")


def farthest_first(me):
    x, y, z, core = me // 32, (me // 8) % 4, (me // 2) % 4, me % 2
    for dx, dy, dz, dc in OFFSETS:
        yield ((x + dx) % 4) * 32 + ((y + dy) % 4) * 8 + ((z + dz) % 4) * 2 + (core + dc) % 2


def start_swap(me, send, recv, send_sem, recv_sem, fill):
    for t in farthest_first(me):
        fill(t)
        pltpu.make_async_remote_copy(
            src_ref=send.at[t], dst_ref=recv.at[me], send_sem=send_sem, recv_sem=recv_sem,
            device_id=place(t), device_id_type=MESH,
        ).start()
    fill(me)
    pltpu.make_async_copy(send.at[me], recv.at[me], recv_sem).start()


def wait_swap(send, recv, send_sem, recv_sem):
    pltpu.make_async_copy(recv, recv, recv_sem).wait()
    others = send.at[pl.ds(0, DEVS - 1)]
    pltpu.make_async_copy(others, others, send_sem).wait()


def spread(block, lane_group):
    return jnp.concatenate([jnp.where(lane_group == g, block, 0.0) for g in range(4)], axis=0).astype(BF16)


def eightfold(e_ref, keep):
    rows = [jnp.where(keep, jnp.broadcast_to(e_ref[c : c + 1, :], (8, 256)), 0.0) for c in range(NB)]
    return jnp.concatenate(rows, axis=0).astype(BF16)


def apply_block(k, w_ref, g, rows, y_ref, where_a, where_c):
    w = jnp.concatenate(
        [
            jnp.concatenate(
                [w_ref[g, rows, where_a(ac, a) * 128 : (where_a(ac, a) + 1) * 128] for a in range(8)], axis=0
            )
            for ac in range(4)
        ],
        axis=1,
    )
    y = jnp.dot(k, w, preferred_element_type=F32)
    for c in range(NB):
        at = where_c(c)
        y_ref[rows, at * 128 : (at + 1) * 128] = jnp.concatenate(
            [y[c * 8 : (c + 1) * 8, ac * 128 : (ac + 1) * 128] for ac in range(4)], axis=0
        ).astype(BF16)


def item_tables(owner_ref, atom_ref, tables):
    items = 2 * PAIRS

    def as_row(ref):
        return jnp.concatenate([ref[0:1, :], ref[1:2, :]], axis=1)

    owner = as_row(owner_ref)
    item = lax.broadcasted_iota(jnp.int32, (items, items), 0)
    across = lax.broadcasted_iota(jnp.int32, (items, items), 1)
    column = jnp.sum(jnp.where(item == across, owner, 0), axis=1, keepdims=True)
    slot = jnp.sum(jnp.where((column == owner) & (item < across), 1, 0), axis=0, keepdims=True)
    named = column == across
    first = jnp.min(jnp.where(named, item, items), axis=0, keepdims=True)
    last = jnp.max(jnp.where(named, item, -1), axis=0, keepdims=True)
    tables[0:1, :] = owner * ATOMS + as_row(atom_ref)
    tables[1:2, :] = owner
    tables[2:3, :] = slot
    tables[3:4, :] = first
    tables[4:5, :] = jnp.where(last > first, last, items)
    tables[5:8, :] = jnp.zeros((3, items), jnp.int32)


def exchange_kernel(
    owner_ref, atom_ref, integrals, metric, density, total,
    tables, scalars, req, dens, outgoing, landed, outbox, returned, rows32, chosen,
    q_buf, m_buf, z_ref, fw, qw, x_even, r_even, x_odd, r_odd, e1_even, e2_even, e1_odd, e2_odd, terms,
    sems, q_sems, m_sems,
):
    me = my_index()

    def load(g, buffer):
        return (
            pltpu.make_async_copy(integrals.at[pl.ds(g * GROUP, GROUP)], q_buf.at[buffer], q_sems.at[buffer]),
            pltpu.make_async_copy(metric.at[pl.ds(g * GROUP, GROUP)], m_buf.at[buffer], m_sems.at[buffer]),
        )

    barrier = pltpu.get_barrier_semaphore()

    for t in farthest_first(me):
        pl.semaphore_signal(barrier, inc=1, device_id=place(t), device_id_type=MESH)
    for g in range(BUFFERS):
        for copy in load(g, g):
            copy.start()
    density_copy = pltpu.make_async_copy(density, dens, sems.at[4])
    density_copy.start()
    item_tables(owner_ref, atom_ref, tables)
    table_copy = pltpu.make_async_copy(tables, scalars, sems.at[5])
    table_copy.start()
    pl.semaphore_wait(barrier, DEVS - 1)

    codes = tables.at[pl.ds(0, 1)]
    pltpu.make_async_copy(codes, req.at[pl.ds(me, 1)], sems.at[0]).start()
    for t in farthest_first(me):
        pltpu.make_async_remote_copy(
            src_ref=codes, dst_ref=req.at[pl.ds(me, 1)], send_sem=sems.at[1], recv_sem=sems.at[0],
            device_id=place(t), device_id_type=MESH,
        ).start()
    terms[2 * PAIRS] = jnp.zeros((8, 128), F32)

    def fit(g, carry):
        buffer = g % BUFFERS
        for copy in load(g, buffer):
            copy.wait()
        for p in range(GROUP):
            rows = slice(p * NB, (p + 1) * NB)
            for c in range(8):
                t = q_buf[buffer, p, :, c * 128 : (c + 1) * 128].T
                y = jnp.dot(t, m_buf[buffer, p], preferred_element_type=F32)
                for j in range(4):
                    m = 4 * c + j
                    at = (j * 8 + c) * PITCH
                    qw[g, rows, m * 128 : (m + 1) * 128] = t[j * NB : (j + 1) * NB]
                    z_ref[p, at : at + NB, :] = y[j * NB : (j + 1) * NB]
            for n in range(NB):
                fw[g, rows, n * 128 : (n + 1) * 128] = z_ref[p, pl.ds(n, NB, stride=PITCH), :].astype(BF16)

        @pl.when(g + BUFFERS < GROUPS)
        def _():
            for copy in load(g + BUFFERS, buffer):
                copy.start()

        return carry

    lax.fori_loop(0, EARLY, fit, 0)

    pltpu.make_async_copy(req, req, sems.at[0]).wait()
    density_copy.wait()
    local = req[...] - ATOMS * me
    mine = (local >= 0) & (local < ATOMS)
    coded = lax.broadcasted_iota(jnp.int32, (DEVS, 128), 1) * 128 + local
    first = jnp.min(jnp.where(mine, coded, 128 * 128 - 1), axis=1, keepdims=True) % 128
    last = jnp.max(jnp.where(mine, coded, 127), axis=1, keepdims=True) % 128
    atoms = lax.broadcasted_iota(jnp.int32, (DEVS, 128), 1)
    onehots = [jnp.where(atoms == atom, 1.0, 0.0) for atom in (first, last)]
    for c in range(2):
        picks = onehots[c][:, :ATOMS].astype(BF16)
        for part in range(8):
            rows32[pl.ds(8 * c + part, DEVS, stride=16), :] = jnp.dot(
                picks, dens[:, part * 128 : (part + 1) * 128], preferred_element_type=F32
            )

    def answer(t):
        outgoing[t] = rows32[pl.ds(pl.multiple_of(t * 16, 16), 16), :].astype(BF16)

    start_swap(me, outgoing, landed, sems.at[2], sems.at[3], answer)
    for c in range(2):
        chosen[c] = onehots[c].T.astype(BF16)
    others = req.at[pl.ds(0, DEVS - 1)]
    pltpu.make_async_copy(others, others, sems.at[1]).wait()
    table_copy.wait()
    lax.fori_loop(EARLY, GROUPS, fit, 0)
    wait_swap(outgoing, landed, sems.at[2], sems.at[3])

    lane256 = lax.broadcasted_iota(jnp.int32, (8, 256), 1)
    keep = lax.broadcasted_iota(jnp.int32, (8, 256), 0) == lane256 // NB
    lane_group = lax.broadcasted_iota(jnp.int32, (8, 128), 1) // NB
    tile8 = jnp.where(
        lax.broadcasted_iota(jnp.int32, (128, 256), 0) % NB == lax.broadcasted_iota(jnp.int32, (128, 256), 1) % NB,
        1.0, 0.0,
    ).astype(BF16)
    pick = jnp.where(
        lax.broadcasted_iota(jnp.int32, (NB, 128), 0) == lax.broadcasted_iota(jnp.int32, (NB, 128), 1) % NB, 1.0, 0.0
    ).astype(BF16)

    def fetched(item):
        both = landed[scalars[1, item]].astype(F32)
        return jnp.where(scalars[2, item] == 0, both[:8], both[8:])

    def expand(g, e1, e2):
        firsts = [spread(fetched(g * GROUP + p), lane_group) for p in range(GROUP)]
        seconds = [spread(fetched(PAIRS + g * GROUP + p), lane_group) for p in range(GROUP)]
        e2[...] = jnp.dot(
            jnp.concatenate(seconds, axis=0), tile8, preferred_element_type=F32
        ).reshape(GROUP, NB, 256)
        wide = lax.dot_general(
            pick, jnp.concatenate([f for f in firsts for _ in range(8)], axis=0), NT, preferred_element_type=F32
        )
        for p in range(GROUP):
            e1[p] = wide[:, p * 256 : (p + 1) * 256]

    def apply(g, e1, e2, x, r):
        for p in range(GROUP):
            rows = slice(p * NB, (p + 1) * NB)
            apply_block(
                eightfold(e2.at[p], keep), qw, g, rows, x, lambda ac, a: ac * 8 + a, lambda c: (c % 8) * 4 + c // 8
            )
            apply_block(eightfold(e1.at[p], keep), fw, g, rows, r, lambda ac, a: a * 4 + ac, lambda c: c)

    def contract(g, x, r):
        first_gram = lax.dot_general(fw[g], x[...], NT, preferred_element_type=F32)
        second_gram = lax.dot_general(r[...], qw[g], NT, preferred_element_type=F32)
        for side, gram in ((0, first_gram), (1, second_gram)):
            for p in range(GROUP):
                block = jnp.zeros((8, 128), F32)
                for k in range(4):
                    part = gram[p * NB + k * 8 : p * NB + (k + 1) * 8, :]
                    turn = ((k - p) % 4) * NB
                    block = jnp.where(lane_group == k, part if turn == 0 else pltpu.roll(part, turn, 1), block)
                terms[side * PAIRS + g * GROUP + p] = block

    expand(0, e1_even, e2_even)
    apply(0, e1_even, e2_even, x_even, r_even)

    def two_groups(h, carry):
        g = 2 * h
        expand(g + 1, e1_odd, e2_odd)
        contract(g, x_even, r_even)
        apply(g + 1, e1_odd, e2_odd, x_odd, r_odd)
        expand(g + 2, e1_even, e2_even)
        contract(g + 1, x_odd, r_odd)
        apply(g + 2, e1_even, e2_even, x_even, r_even)
        return carry

    lax.fori_loop(0, GROUPS // 2 - 1, two_groups, 0)
    expand(GROUPS - 1, e1_odd, e2_odd)
    contract(GROUPS - 2, x_even, r_even)
    apply(GROUPS - 1, e1_odd, e2_odd, x_odd, r_odd)
    contract(GROUPS - 1, x_odd, r_odd)

    def box(t):
        outbox[t] = jnp.concatenate([terms[scalars[3, t]], terms[scalars[4, t]]], axis=0).astype(BF16)

    start_swap(me, outbox, returned, sems.at[6], sems.at[7], box)
    wait_swap(outbox, returned, sems.at[6], sems.at[7])
    rows32[...] = returned[...].astype(F32).reshape(DEVS * 16, 128)
    for part in range(8):
        acc = None
        for c in range(2):
            tile = rows32[pl.ds(8 * c + part, DEVS, stride=16), :].astype(BF16)
            term = jnp.dot(chosen[c, :ATOMS, :], tile, preferred_element_type=F32)
            acc = term if acc is None else acc + term
        total[:, part * 128 : (part + 1) * 128] = acc


def local(pair_owner, pair_atom, integrals, metric_inverse, density):
    vmem = pl.BlockSpec(memory_space=pltpu.VMEM)
    hbm = pl.BlockSpec(memory_space=pl.ANY)
    boxes = pltpu.VMEM((DEVS, 16, 128), BF16)
    wide = (GROUP * NB, NB * NFIT)
    return pl.pallas_call(
        exchange_kernel,
        out_shape=jax.ShapeDtypeStruct((ATOMS, NB * NB), F32),
        in_specs=[vmem, vmem, hbm, hbm, hbm],
        out_specs=vmem,
        scratch_shapes=[
            pltpu.VMEM((8, 2 * PAIRS), jnp.int32),
            pltpu.SMEM((8, 2 * PAIRS), jnp.int32),
            pltpu.VMEM((DEVS, 2 * PAIRS), jnp.int32),
            pltpu.VMEM((ATOMS, NB * NB), BF16),
            boxes, boxes, boxes, boxes,
            pltpu.VMEM((DEVS * 16, 128), F32),
            pltpu.VMEM((2, 128, DEVS), BF16),
            pltpu.VMEM((BUFFERS, GROUP, NFIT, NB * NB), BF16),
            pltpu.VMEM((BUFFERS, GROUP, NFIT, NFIT), BF16),
            pltpu.VMEM((GROUP, NB * PITCH, 128), F32),
            pltpu.VMEM((GROUPS, *wide), BF16),
            pltpu.VMEM((GROUPS, *wide), BF16),
            *[pltpu.VMEM(wide, BF16)] * 4,
            *[pltpu.VMEM((GROUP, NB, 256), F32)] * 4,
            pltpu.VMEM((2 * PAIRS + 1, 8, 128), F32),
            pltpu.SemaphoreType.DMA((8,)),
            pltpu.SemaphoreType.DMA((BUFFERS,)),
            pltpu.SemaphoreType.DMA((BUFFERS,)),
        ],
        compiler_params=pltpu.CompilerParams(
            collective_id=0, has_side_effects=True, vmem_limit_bytes=58 * 2**20
        ),
        name="exchange",
    )(pair_owner.T, pair_atom.T, integrals, metric_inverse, density)


def solution(mesh):
    placed = (
        P(("grp", "dev"), None),
        P(("grp", "dev"), None),
        P(("grp", "dev"), None, None),
        P(("grp", "dev"), None, None),
        P(("grp", "dev"), None),
    )
    return jax.shard_map(
        local, mesh=mesh, in_specs=placed, out_specs=P(("grp", "dev"), None), check_vma=False
    )
```

```python
import itertools

import jax
import jax.numpy as jnp
from jax import lax
from jax.experimental import pallas as pl
from jax.experimental.pallas import tpu as pltpu
from jax.sharding import PartitionSpec as P

NB = 32
NFIT = 128
ATOMS = 96
PAIRS = 64
DEVS = 128
GROUP = 4
GROUPS = PAIRS // GROUP
BUFFERS = 4
EARLY = 6
BOX = 24
PITCH = 33
BF16 = jnp.bfloat16
F32 = jnp.float32
MESH = pl.DeviceIdType.MESH
NT = (((1,), (1,)), ((), ()))


OFFSETS = sorted(
    (o for o in itertools.product(range(4), range(4), range(4), range(2)) if any(o)),
    key=lambda o: (-sum(min(v, 4 - v) for v in o[:3]), -o[3]),
)


def place(t):
    return (t // 32, t % 32)


def my_index():
    return lax.axis_index("grp") * 32 + lax.axis_index("dev")


def farthest_first(me):
    x, y, z, core = me // 32, (me // 8) % 4, (me // 2) % 4, me % 2
    for dx, dy, dz, dc in OFFSETS:
        yield ((x + dx) % 4) * 32 + ((y + dy) % 4) * 8 + ((z + dz) % 4) * 2 + (core + dc) % 2


def start_swap(me, send, recv, send_sem, recv_sem, fill):
    for t in farthest_first(me):
        fill(t)
        pltpu.make_async_remote_copy(
            src_ref=send.at[t], dst_ref=recv.at[me], send_sem=send_sem, recv_sem=recv_sem,
            device_id=place(t), device_id_type=MESH,
        ).start()
    fill(me)
    pltpu.make_async_copy(send.at[me], recv.at[me], recv_sem).start()


def wait_received(recv, recv_sem):
    pltpu.make_async_copy(recv, recv, recv_sem).wait()


def wait_sent(send, send_sem):
    others = send.at[pl.ds(0, DEVS - 1)]
    pltpu.make_async_copy(others, others, send_sem).wait()


def spread(block, lane_group):
    return jnp.concatenate([jnp.where(lane_group == g, block, 0.0) for g in range(4)], axis=0).astype(BF16)


def eightfold(e_ref, keep):
    rows = [jnp.where(keep, jnp.broadcast_to(e_ref[c : c + 1, :], (8, 256)), 0.0) for c in range(NB)]
    return jnp.concatenate(rows, axis=0).astype(BF16)


def apply_block(k, w_ref, g, rows, y_ref, where_a, where_c):
    w = jnp.concatenate(
        [
            jnp.concatenate(
                [w_ref[g, rows, where_a(ac, a) * 128 : (where_a(ac, a) + 1) * 128] for a in range(8)], axis=0
            )
            for ac in range(4)
        ],
        axis=1,
    )
    y = jnp.dot(k, w, preferred_element_type=F32)
    for c in range(NB):
        at = where_c(c)
        y_ref[rows, at * 128 : (at + 1) * 128] = jnp.concatenate(
            [y[c * 8 : (c + 1) * 8, ac * 128 : (ac + 1) * 128] for ac in range(4)], axis=0
        ).astype(BF16)


def item_tables(owner_ref, atom_ref, tables):
    items = 2 * PAIRS

    def as_row(ref):
        return jnp.concatenate([ref[0:1, :], ref[1:2, :]], axis=1)

    owner = as_row(owner_ref)
    item = lax.broadcasted_iota(jnp.int32, (items, items), 0)
    across = lax.broadcasted_iota(jnp.int32, (items, items), 1)
    column = jnp.sum(jnp.where(item == across, owner, 0), axis=1, keepdims=True)
    slot = jnp.sum(jnp.where((column == owner) & (item < across), 1, 0), axis=0, keepdims=True)
    named = column == across
    first = jnp.min(jnp.where(named, item, items), axis=0, keepdims=True)
    last = jnp.max(jnp.where(named, item, -1), axis=0, keepdims=True)
    tables[0:1, :] = owner * ATOMS + as_row(atom_ref)
    tables[1:2, :] = owner
    tables[2:3, :] = slot
    tables[3:4, :] = first
    tables[4:5, :] = jnp.where(last > first, last, items)
    tables[5:8, :] = jnp.zeros((3, items), jnp.int32)


def exchange_kernel(
    owners, atoms, integrals, metric, density, total,
    owner_ref, atom_ref, tables, scalars, req, dens, outgoing, landed, outbox, returned, rows32, chosen,
    q_buf, m_buf, z_ref, fw, qw, x_even, r_even, x_odd, r_odd, e1_even, e2_even, e1_odd, e2_odd, terms,
    sems, index_sems, q_sems, m_sems,
):
    me = my_index()

    def load(g, buffer):
        return (
            pltpu.make_async_copy(integrals.at[pl.ds(g * GROUP, GROUP)], q_buf.at[buffer], q_sems.at[buffer]),
            pltpu.make_async_copy(metric.at[pl.ds(g * GROUP, GROUP)], m_buf.at[buffer], m_sems.at[buffer]),
        )

    index_copies = [
        pltpu.make_async_copy(owners, owner_ref, index_sems.at[0]),
        pltpu.make_async_copy(atoms, atom_ref, index_sems.at[1]),
    ]
    for copy in index_copies:
        copy.start()
    barrier = pltpu.get_barrier_semaphore()

    for t in farthest_first(me):
        pl.semaphore_signal(barrier, inc=1, device_id=place(t), device_id_type=MESH)
    for g in range(BUFFERS):
        for copy in load(g, g):
            copy.start()
    density_copy = pltpu.make_async_copy(density, dens, sems.at[4])
    density_copy.start()
    for copy in index_copies:
        copy.wait()
    item_tables(owner_ref, atom_ref, tables)
    table_copy = pltpu.make_async_copy(tables, scalars, sems.at[5])
    table_copy.start()
    pl.semaphore_wait(barrier, DEVS - 1)

    codes = tables.at[pl.ds(0, 1)]
    pltpu.make_async_copy(codes, req.at[pl.ds(me, 1)], sems.at[0]).start()
    for t in farthest_first(me):
        pltpu.make_async_remote_copy(
            src_ref=codes, dst_ref=req.at[pl.ds(me, 1)], send_sem=sems.at[1], recv_sem=sems.at[0],
            device_id=place(t), device_id_type=MESH,
        ).start()
    terms[2 * PAIRS] = jnp.zeros((8, 128), F32)

    def fit(g, carry):
        buffer = g % BUFFERS
        for copy in load(g, buffer):
            copy.wait()
        for p in range(GROUP):
            rows = slice(p * NB, (p + 1) * NB)
            for c in range(8):
                t = q_buf[buffer, p, :, c * 128 : (c + 1) * 128].T
                y = jnp.dot(t, m_buf[buffer, p], preferred_element_type=F32)
                for j in range(4):
                    m = 4 * c + j
                    at = (j * 8 + c) * PITCH
                    qw[g, rows, m * 128 : (m + 1) * 128] = t[j * NB : (j + 1) * NB]
                    z_ref[p, at : at + NB, :] = y[j * NB : (j + 1) * NB]
            for n in range(NB):
                fw[g, rows, n * 128 : (n + 1) * 128] = z_ref[p, pl.ds(n, NB, stride=PITCH), :].astype(BF16)

        @pl.when(g + BUFFERS < GROUPS)
        def _():
            for copy in load(g + BUFFERS, buffer):
                copy.start()

        return carry

    lax.fori_loop(0, EARLY, fit, 0)

    wait_received(req, sems.at[0])
    density_copy.wait()
    local = req[...] - ATOMS * me
    mine = (local >= 0) & (local < ATOMS)
    coded = lax.broadcasted_iota(jnp.int32, (DEVS, 128), 1) * 128 + local
    first = jnp.min(jnp.where(mine, coded, 128 * 128 - 1), axis=1, keepdims=True) % 128
    last = jnp.max(jnp.where(mine, coded, 127), axis=1, keepdims=True) % 128
    local_atom = lax.broadcasted_iota(jnp.int32, (DEVS, 128), 1)
    onehots = [jnp.where(local_atom == atom, 1.0, 0.0) for atom in (first, last)]
    for c in range(2):
        picks = onehots[c][:, :ATOMS].astype(BF16)
        for part in range(8):
            rows32[pl.ds(8 * c + part, DEVS, stride=BOX), :] = jnp.dot(
                picks, dens[:, part * 128 : (part + 1) * 128], preferred_element_type=F32
            )

    def answer(t):
        outgoing[t] = rows32[pl.ds(pl.multiple_of(t * BOX, 8), 16), :].astype(BF16)

    start_swap(me, outgoing, landed, sems.at[2], sems.at[3], answer)
    for c in range(2):
        chosen[c] = onehots[c].T.astype(BF16)
    table_copy.wait()
    lax.fori_loop(EARLY, GROUPS, fit, 0)
    wait_received(landed, sems.at[3])

    lane256 = lax.broadcasted_iota(jnp.int32, (8, 256), 1)
    keep = lax.broadcasted_iota(jnp.int32, (8, 256), 0) == lane256 // NB
    lane_group = lax.broadcasted_iota(jnp.int32, (8, 128), 1) // NB
    tile8 = jnp.where(
        lax.broadcasted_iota(jnp.int32, (128, 256), 0) % NB == lax.broadcasted_iota(jnp.int32, (128, 256), 1) % NB,
        1.0, 0.0,
    ).astype(BF16)
    pick = jnp.where(
        lax.broadcasted_iota(jnp.int32, (NB, 128), 0) == lax.broadcasted_iota(jnp.int32, (NB, 128), 1) % NB, 1.0, 0.0
    ).astype(BF16)

    def fetched(item):
        both = landed[scalars[1, item]].astype(F32)
        return jnp.where(scalars[2, item] == 0, both[:8], both[8:])

    def expand(g, e1, e2):
        firsts = [spread(fetched(g * GROUP + p), lane_group) for p in range(GROUP)]
        seconds = [spread(fetched(PAIRS + g * GROUP + p), lane_group) for p in range(GROUP)]
        e2[...] = jnp.dot(
            jnp.concatenate(seconds, axis=0), tile8, preferred_element_type=F32
        ).reshape(GROUP, NB, 256)
        wide = lax.dot_general(
            pick, jnp.concatenate([f for f in firsts for _ in range(8)], axis=0), NT, preferred_element_type=F32
        )
        for p in range(GROUP):
            e1[p] = wide[:, p * 256 : (p + 1) * 256]

    def apply(g, e1, e2, x, r):
        for p in range(GROUP):
            rows = slice(p * NB, (p + 1) * NB)
            apply_block(
                eightfold(e2.at[p], keep), qw, g, rows, x, lambda ac, a: ac * 8 + a, lambda c: (c % 8) * 4 + c // 8
            )
            apply_block(eightfold(e1.at[p], keep), fw, g, rows, r, lambda ac, a: a * 4 + ac, lambda c: c)

    def contract(g, x, r):
        first_gram = lax.dot_general(fw[g], x[...], NT, preferred_element_type=F32)
        second_gram = lax.dot_general(r[...], qw[g], NT, preferred_element_type=F32)
        for side, gram in ((0, first_gram), (1, second_gram)):
            for p in range(GROUP):
                block = jnp.zeros((8, 128), F32)
                for k in range(4):
                    part = gram[p * NB + k * 8 : p * NB + (k + 1) * 8, :]
                    turn = ((k - p) % 4) * NB
                    block = jnp.where(lane_group == k, part if turn == 0 else pltpu.roll(part, turn, 1), block)
                terms[side * PAIRS + g * GROUP + p] = block

    expand(0, e1_even, e2_even)
    apply(0, e1_even, e2_even, x_even, r_even)

    def two_groups(h, carry):
        g = 2 * h
        expand(g + 1, e1_odd, e2_odd)
        contract(g, x_even, r_even)
        apply(g + 1, e1_odd, e2_odd, x_odd, r_odd)
        expand(g + 2, e1_even, e2_even)
        contract(g + 1, x_odd, r_odd)
        apply(g + 2, e1_even, e2_even, x_even, r_even)
        return carry

    lax.fori_loop(0, GROUPS // 2 - 1, two_groups, 0)
    expand(GROUPS - 1, e1_odd, e2_odd)
    contract(GROUPS - 2, x_even, r_even)
    apply(GROUPS - 1, e1_odd, e2_odd, x_odd, r_odd)
    contract(GROUPS - 1, x_odd, r_odd)

    def box(t):
        outbox[t] = jnp.concatenate([terms[scalars[3, t]], terms[scalars[4, t]]], axis=0).astype(BF16)

    start_swap(me, outbox, returned, sems.at[6], sems.at[7], box)
    wait_received(returned, sems.at[7])
    for t in range(DEVS):
        rows32[t * BOX : t * BOX + 16, :] = returned[t].astype(F32)
    for part in range(8):
        acc = None
        for c in range(2):
            tile = rows32[pl.ds(8 * c + part, DEVS, stride=BOX), :].astype(BF16)
            term = jnp.dot(chosen[c, :ATOMS, :], tile, preferred_element_type=F32)
            acc = term if acc is None else acc + term
        total[:, part * 128 : (part + 1) * 128] = acc
    wait_sent(req, sems.at[1])
    wait_sent(outgoing, sems.at[2])
    wait_sent(outbox, sems.at[6])


def local(pair_owner, pair_atom, integrals, metric_inverse, density):
    vmem = pl.BlockSpec(memory_space=pltpu.VMEM)
    hbm = pl.BlockSpec(memory_space=pltpu.HBM)
    boxes = pltpu.VMEM((DEVS, 16, 128), BF16)
    wide = (GROUP * NB, NB * NFIT)
    return pl.pallas_call(
        exchange_kernel,
        out_shape=jax.ShapeDtypeStruct((ATOMS, NB * NB), F32),
        in_specs=[hbm] * 5,
        out_specs=vmem,
        scratch_shapes=[
            pltpu.VMEM((2, PAIRS), jnp.int32),
            pltpu.VMEM((2, PAIRS), jnp.int32),
            pltpu.VMEM((8, 2 * PAIRS), jnp.int32),
            pltpu.SMEM((8, 2 * PAIRS), jnp.int32),
            pltpu.VMEM((DEVS, 2 * PAIRS), jnp.int32),
            pltpu.VMEM((ATOMS, NB * NB), BF16),
            boxes, boxes, boxes, boxes,
            pltpu.VMEM((DEVS * BOX, 128), F32),
            pltpu.VMEM((2, 128, DEVS), BF16),
            pltpu.VMEM((BUFFERS, GROUP, NFIT, NB * NB), BF16),
            pltpu.VMEM((BUFFERS, GROUP, NFIT, NFIT), BF16),
            pltpu.VMEM((GROUP, NB * PITCH, 128), F32),
            pltpu.VMEM((GROUPS, *wide), BF16),
            pltpu.VMEM((GROUPS, *wide), BF16),
            *[pltpu.VMEM(wide, BF16)] * 4,
            *[pltpu.VMEM((GROUP, NB, 256), F32)] * 4,
            pltpu.VMEM((2 * PAIRS + 1, 8, 128), F32),
            pltpu.SemaphoreType.DMA((8,)),
            pltpu.SemaphoreType.DMA((2,)),
            pltpu.SemaphoreType.DMA((BUFFERS,)),
            pltpu.SemaphoreType.DMA((BUFFERS,)),
        ],
        compiler_params=pltpu.CompilerParams(
            collective_id=0, has_side_effects=True, vmem_limit_bytes=58 * 2**20
        ),
        name="exchange",
    )(pair_owner.T, pair_atom.T, integrals, metric_inverse, density)


def solution(mesh):
    placed = (
        P(("grp", "dev"), None),
        P(("grp", "dev"), None),
        P(("grp", "dev"), None, None),
        P(("grp", "dev"), None, None),
        P(("grp", "dev"), None),
    )
    return jax.shard_map(
        local, mesh=mesh, in_specs=placed, out_specs=P(("grp", "dev"), None), check_vma=False
    )
```

```python
import itertools

import jax
import jax.numpy as jnp
from jax import lax
from jax.experimental import pallas as pl
from jax.experimental.pallas import tpu as pltpu
from jax.sharding import PartitionSpec as P

NB = 32
NFIT = 128
ATOMS = 96
PAIRS = 64
DEVS = 128
GROUP = 4
GROUPS = PAIRS // GROUP
BUFFERS = 4
EARLY = 6
BOX = 24
PITCH = 33
BF16 = jnp.bfloat16
F32 = jnp.float32
MESH = pl.DeviceIdType.MESH
NT = (((1,), (1,)), ((), ()))


OFFSETS = sorted(
    (o for o in itertools.product(range(4), range(4), range(4), range(2)) if any(o)),
    key=lambda o: (-sum(min(v, 4 - v) for v in o[:3]), -o[3]),
)


def place(t):
    return (t // 32, t % 32)


def my_index():
    return lax.axis_index("grp") * 32 + lax.axis_index("dev")


def farthest_first(me):
    x, y, z, core = me // 32, (me // 8) % 4, (me // 2) % 4, me % 2
    for dx, dy, dz, dc in OFFSETS:
        yield ((x + dx) % 4) * 32 + ((y + dy) % 4) * 8 + ((z + dz) % 4) * 2 + (core + dc) % 2


def start_swap(me, send, recv, send_sem, recv_sem, fill):
    for t in farthest_first(me):
        fill(t)
        pltpu.make_async_remote_copy(
            src_ref=send.at[t], dst_ref=recv.at[me], send_sem=send_sem, recv_sem=recv_sem,
            device_id=place(t), device_id_type=MESH,
        ).start()
    fill(me)
    pltpu.make_async_copy(send.at[me], recv.at[me], recv_sem).start()


def wait_received(recv, recv_sem):
    pltpu.make_async_copy(recv, recv, recv_sem).wait()


def wait_sent(send, send_sem):
    others = send.at[pl.ds(0, DEVS - 1)]
    pltpu.make_async_copy(others, others, send_sem).wait()


def spread(block, lane_group):
    return jnp.concatenate([jnp.where(lane_group == g, block, 0.0) for g in range(4)], axis=0).astype(BF16)


def eightfold(e_ref, keep):
    rows = [jnp.where(keep, jnp.broadcast_to(e_ref[c : c + 1, :], (8, 256)), 0.0) for c in range(NB)]
    return jnp.concatenate(rows, axis=0).astype(BF16)


def apply_block(k, w_ref, g, rows, y_ref, where_a, where_c):
    w = jnp.concatenate(
        [
            jnp.concatenate(
                [w_ref[g, rows, where_a(ac, a) * 128 : (where_a(ac, a) + 1) * 128] for a in range(8)], axis=0
            )
            for ac in range(4)
        ],
        axis=1,
    )
    y = jnp.dot(k, w, preferred_element_type=F32)
    for c in range(NB):
        at = where_c(c)
        y_ref[rows, at * 128 : (at + 1) * 128] = jnp.concatenate(
            [y[c * 8 : (c + 1) * 8, ac * 128 : (ac + 1) * 128] for ac in range(4)], axis=0
        ).astype(BF16)


def item_tables(owner_ref, atom_ref, tables):
    items = 2 * PAIRS

    def as_row(ref):
        return jnp.concatenate([ref[0:1, :], ref[1:2, :]], axis=1)

    owner = as_row(owner_ref)
    item = lax.broadcasted_iota(jnp.int32, (items, items), 0)
    across = lax.broadcasted_iota(jnp.int32, (items, items), 1)
    column = jnp.sum(jnp.where(item == across, owner, 0), axis=1, keepdims=True)
    slot = jnp.sum(jnp.where((column == owner) & (item < across), 1, 0), axis=0, keepdims=True)
    named = column == across
    first = jnp.min(jnp.where(named, item, items), axis=0, keepdims=True)
    last = jnp.max(jnp.where(named, item, -1), axis=0, keepdims=True)
    tables[0:1, :] = owner * ATOMS + as_row(atom_ref)
    tables[1:2, :] = owner
    tables[2:3, :] = slot
    tables[3:4, :] = first
    tables[4:5, :] = jnp.where(last > first, last, items)
    tables[5:8, :] = jnp.zeros((3, items), jnp.int32)


def exchange_kernel(
    owners, atoms, integrals, metric, density, total,
    owner_ref, atom_ref, tables, scalars, req, dens, outgoing, landed, outbox, returned, rows32, chosen, summed,
    q_buf, m_buf, z_ref, fw, qw, x_even, r_even, x_odd, r_odd, e1_even, e2_even, e1_odd, e2_odd, terms,
    sems, out_sems, index_sems, q_sems, m_sems,
):
    me = my_index()

    def load(g, buffer):
        return (
            pltpu.make_async_copy(integrals.at[pl.ds(g * GROUP, GROUP)], q_buf.at[buffer], q_sems.at[buffer]),
            pltpu.make_async_copy(metric.at[pl.ds(g * GROUP, GROUP)], m_buf.at[buffer], m_sems.at[buffer]),
        )

    index_copies = [
        pltpu.make_async_copy(owners, owner_ref, index_sems.at[0]),
        pltpu.make_async_copy(atoms, atom_ref, index_sems.at[1]),
    ]
    for copy in index_copies:
        copy.start()
    barrier = pltpu.get_barrier_semaphore()

    for t in farthest_first(me):
        pl.semaphore_signal(barrier, inc=1, device_id=place(t), device_id_type=MESH)
    for g in range(BUFFERS):
        for copy in load(g, g):
            copy.start()
    density_copy = pltpu.make_async_copy(density, dens, sems.at[4])
    density_copy.start()
    for copy in index_copies:
        copy.wait()
    item_tables(owner_ref, atom_ref, tables)
    table_copy = pltpu.make_async_copy(tables, scalars, sems.at[5])
    table_copy.start()
    pl.semaphore_wait(barrier, DEVS - 1)

    codes = tables.at[pl.ds(0, 1)]
    pltpu.make_async_copy(codes, req.at[pl.ds(me, 1)], sems.at[0]).start()
    for t in farthest_first(me):
        pltpu.make_async_remote_copy(
            src_ref=codes, dst_ref=req.at[pl.ds(me, 1)], send_sem=sems.at[1], recv_sem=sems.at[0],
            device_id=place(t), device_id_type=MESH,
        ).start()
    terms[2 * PAIRS] = jnp.zeros((8, 128), F32)

    def fit(g, carry):
        buffer = g % BUFFERS
        for copy in load(g, buffer):
            copy.wait()
        for p in range(GROUP):
            rows = slice(p * NB, (p + 1) * NB)
            for c in range(8):
                t = q_buf[buffer, p, :, c * 128 : (c + 1) * 128].T
                y = jnp.dot(t, m_buf[buffer, p], preferred_element_type=F32)
                for j in range(4):
                    m = 4 * c + j
                    at = (j * 8 + c) * PITCH
                    qw[g, rows, m * 128 : (m + 1) * 128] = t[j * NB : (j + 1) * NB]
                    z_ref[p, at : at + NB, :] = y[j * NB : (j + 1) * NB]
            for n in range(NB):
                fw[g, rows, n * 128 : (n + 1) * 128] = z_ref[p, pl.ds(n, NB, stride=PITCH), :].astype(BF16)

        @pl.when(g + BUFFERS < GROUPS)
        def _():
            for copy in load(g + BUFFERS, buffer):
                copy.start()

        return carry

    lax.fori_loop(0, EARLY, fit, 0)

    wait_received(req, sems.at[0])
    density_copy.wait()
    local = req[...] - ATOMS * me
    mine = (local >= 0) & (local < ATOMS)
    coded = lax.broadcasted_iota(jnp.int32, (DEVS, 128), 1) * 128 + local
    first = jnp.min(jnp.where(mine, coded, 128 * 128 - 1), axis=1, keepdims=True) % 128
    last = jnp.max(jnp.where(mine, coded, 127), axis=1, keepdims=True) % 128
    local_atom = lax.broadcasted_iota(jnp.int32, (DEVS, 128), 1)
    onehots = [jnp.where(local_atom == atom, 1.0, 0.0) for atom in (first, last)]
    for c in range(2):
        picks = onehots[c][:, :ATOMS].astype(BF16)
        picked = jnp.dot(picks, dens[...], preferred_element_type=F32)
        for part in range(8):
            rows32[pl.ds(8 * c + part, DEVS, stride=BOX), :] = picked[:, part * 128 : (part + 1) * 128]

    def answer(t):
        outgoing[t] = rows32[pl.ds(pl.multiple_of(t * BOX, 8), 16), :].astype(BF16)

    start_swap(me, outgoing, landed, sems.at[2], sems.at[3], answer)
    for c in range(2):
        chosen[:, c * DEVS : (c + 1) * DEVS] = onehots[c].T.astype(BF16)
    table_copy.wait()
    lax.fori_loop(EARLY, GROUPS, fit, 0)
    wait_received(landed, sems.at[3])

    lane256 = lax.broadcasted_iota(jnp.int32, (8, 256), 1)
    keep = lax.broadcasted_iota(jnp.int32, (8, 256), 0) == lane256 // NB
    lane_group = lax.broadcasted_iota(jnp.int32, (8, 128), 1) // NB
    tile8 = jnp.where(
        lax.broadcasted_iota(jnp.int32, (128, 256), 0) % NB == lax.broadcasted_iota(jnp.int32, (128, 256), 1) % NB,
        1.0, 0.0,
    ).astype(BF16)
    pick = jnp.where(
        lax.broadcasted_iota(jnp.int32, (NB, 128), 0) == lax.broadcasted_iota(jnp.int32, (NB, 128), 1) % NB, 1.0, 0.0
    ).astype(BF16)

    def fetched(item):
        both = landed[scalars[1, item]].astype(F32)
        return jnp.where(scalars[2, item] == 0, both[:8], both[8:])

    def expand(g, e1, e2):
        firsts = [spread(fetched(g * GROUP + p), lane_group) for p in range(GROUP)]
        seconds = [spread(fetched(PAIRS + g * GROUP + p), lane_group) for p in range(GROUP)]
        e2[...] = jnp.dot(
            jnp.concatenate(seconds, axis=0), tile8, preferred_element_type=F32
        ).reshape(GROUP, NB, 256)
        wide = lax.dot_general(
            pick, jnp.concatenate([f for f in firsts for _ in range(8)], axis=0), NT, preferred_element_type=F32
        )
        for p in range(GROUP):
            e1[p] = wide[:, p * 256 : (p + 1) * 256]

    def apply(g, e1, e2, x, r):
        for p in range(GROUP):
            rows = slice(p * NB, (p + 1) * NB)
            apply_block(
                eightfold(e2.at[p], keep), qw, g, rows, x, lambda ac, a: ac * 8 + a, lambda c: (c % 8) * 4 + c // 8
            )
            apply_block(eightfold(e1.at[p], keep), fw, g, rows, r, lambda ac, a: a * 4 + ac, lambda c: c)

    def contract(g, x, r):
        first_gram = lax.dot_general(fw[g], x[...], NT, preferred_element_type=F32)
        second_gram = lax.dot_general(r[...], qw[g], NT, preferred_element_type=F32)
        for side, gram in ((0, first_gram), (1, second_gram)):
            for p in range(GROUP):
                block = jnp.zeros((8, 128), F32)
                for k in range(4):
                    part = gram[p * NB + k * 8 : p * NB + (k + 1) * 8, :]
                    turn = ((k - p) % 4) * NB
                    block = jnp.where(lane_group == k, part if turn == 0 else pltpu.roll(part, turn, 1), block)
                terms[side * PAIRS + g * GROUP + p] = block

    expand(0, e1_even, e2_even)
    apply(0, e1_even, e2_even, x_even, r_even)

    def two_groups(h, carry):
        g = 2 * h
        expand(g + 1, e1_odd, e2_odd)
        contract(g, x_even, r_even)
        apply(g + 1, e1_odd, e2_odd, x_odd, r_odd)
        expand(g + 2, e1_even, e2_even)
        contract(g + 1, x_odd, r_odd)
        apply(g + 2, e1_even, e2_even, x_even, r_even)
        return carry

    lax.fori_loop(0, GROUPS // 2 - 2, two_groups, 0, unroll=2)
    two_groups(GROUPS // 2 - 2, 0)
    expand(GROUPS - 1, e1_odd, e2_odd)
    contract(GROUPS - 2, x_even, r_even)
    apply(GROUPS - 1, e1_odd, e2_odd, x_odd, r_odd)
    contract(GROUPS - 1, x_odd, r_odd)

    def box(t):
        outbox[t] = jnp.concatenate([terms[scalars[3, t]], terms[scalars[4, t]]], axis=0).astype(BF16)

    start_swap(me, outbox, returned, sems.at[6], sems.at[7], box)
    wait_received(returned, sems.at[7])

    def out_copy(part):
        columns = pl.ds(part * 128, 128)
        return pltpu.make_async_copy(summed.at[:, columns], total.at[:, columns], out_sems.at[part])

    for t in range(DEVS):
        rows32[t * BOX : t * BOX + 16, :] = returned[t].astype(F32)
    for part in range(8):
        tiles = [rows32[pl.ds(8 * c + part, DEVS, stride=BOX), :].astype(BF16) for c in range(2)]
        summed[:, part * 128 : (part + 1) * 128] = jnp.dot(
            chosen[:ATOMS, :], jnp.concatenate(tiles, axis=0), preferred_element_type=F32
        )
        out_copy(part).start()
    for part in range(8):
        out_copy(part).wait()
    wait_sent(req, sems.at[1])
    wait_sent(outgoing, sems.at[2])
    wait_sent(outbox, sems.at[6])


def local(pair_owner, pair_atom, integrals, metric_inverse, density):
    hbm = pl.BlockSpec(memory_space=pltpu.HBM)
    boxes = pltpu.VMEM((DEVS, 16, 128), BF16)
    wide = (GROUP * NB, NB * NFIT)
    return pl.pallas_call(
        exchange_kernel,
        out_shape=jax.ShapeDtypeStruct((ATOMS, NB * NB), F32),
        in_specs=[hbm] * 5,
        out_specs=hbm,
        scratch_shapes=[
            pltpu.VMEM((2, PAIRS), jnp.int32),
            pltpu.VMEM((2, PAIRS), jnp.int32),
            pltpu.VMEM((8, 2 * PAIRS), jnp.int32),
            pltpu.SMEM((8, 2 * PAIRS), jnp.int32),
            pltpu.VMEM((DEVS, 2 * PAIRS), jnp.int32),
            pltpu.VMEM((ATOMS, NB * NB), BF16),
            boxes, boxes, boxes, boxes,
            pltpu.VMEM((DEVS * BOX, 128), F32),
            pltpu.VMEM((128, 2 * DEVS), BF16),
            pltpu.VMEM((ATOMS, NB * NB), F32),
            pltpu.VMEM((BUFFERS, GROUP, NFIT, NB * NB), BF16),
            pltpu.VMEM((BUFFERS, GROUP, NFIT, NFIT), BF16),
            pltpu.VMEM((GROUP, NB * PITCH, 128), F32),
            pltpu.VMEM((GROUPS, *wide), BF16),
            pltpu.VMEM((GROUPS, *wide), BF16),
            *[pltpu.VMEM(wide, BF16)] * 4,
            *[pltpu.VMEM((GROUP, NB, 256), F32)] * 4,
            pltpu.VMEM((2 * PAIRS + 1, 8, 128), F32),
            pltpu.SemaphoreType.DMA((8,)),
            pltpu.SemaphoreType.DMA((8,)),
            pltpu.SemaphoreType.DMA((2,)),
            pltpu.SemaphoreType.DMA((BUFFERS,)),
            pltpu.SemaphoreType.DMA((BUFFERS,)),
        ],
        compiler_params=pltpu.CompilerParams(
            collective_id=0, has_side_effects=True, vmem_limit_bytes=58 * 2**20
        ),
        name="exchange",
    )(pair_owner.T, pair_atom.T, integrals, metric_inverse, density)


def solution(mesh):
    placed = (
        P(("grp", "dev"), None),
        P(("grp", "dev"), None),
        P(("grp", "dev"), None, None),
        P(("grp", "dev"), None, None),
        P(("grp", "dev"), None),
    )
    return jax.shard_map(
        local, mesh=mesh, in_specs=placed, out_specs=P(("grp", "dev"), None), check_vma=False
    )
```
